768 devices in a mesh: row: 8 (over y_hi, x), col: 96 (over y_lo, z, core).
Axes of the slice: x: 4, y: 8 (y_hi: 2, y_lo: 4; y = y_hi * 4 + y_lo), z: 12, core: 2. Of those that a mesh axis runs over, the one named last changes fastest.
Arguments:
- grad: bfloat16 [3072, 3072], P('row', 'col'), may hold values from -6 to 6
- left_rows: bfloat16 [3072, 3072], P('col', 'row'), may hold values from -0.109375 to 0.109375
- right_basis: bfloat16 [3072, 3072], P('col', 'row'), may hold values from -0.109375 to 0.109375
- first: float32 [3072, 3072], P('row', 'col'), may hold values from -6 to 6
- second: float32 [3072, 3072], P('row', 'col'), may hold values from 0.05 to 4
Outputs:
- update: bfloat16 [3072, 3072], P('row', 'col')
- first_out: float32 [3072, 3072], P('row', 'col')
- second_out: float32 [3072, 3072], P('row', 'col')
The draws below stay inside these ranges and needn't reach their ends.
All inputs are finite; a program needn't handle non-finite values.
Results may differ from the reference program's by a relative error of at most 0.022.
Values may be sent and summed in bfloat16 or wider, within the bound.
A program may use at most 32 MiB of HBM per device.

```python
import math
import jax
import jax.numpy as jnp
from jax import lax

D = 3072
N_ROW = 8


def levels(stream_key, extent, cuts, low, largest):
    level = 1.0
    for position, shards_of in cuts:
        steps = jax.random.uniform(jax.random.fold_in(jax.random.fold_in(stream_key, 6), position), (shards_of,), jnp.float32, low / len(cuts), largest / len(cuts))
        level = level * jnp.repeat(jnp.exp(steps), extent[position] // shards_of).reshape((-1,) + (1,) * (len(extent) - 1 - position))
    return level


def scatter_about(stream_key, extent, spread, reach, pieces=(), dtype=jnp.bfloat16):
    loudness = levels(stream_key, extent, pieces, -0.22, 0.18) if pieces else 1.0
    result = jax.random.normal(stream_key, extent, jnp.float32) * spread * loudness
    return jnp.minimum(jnp.maximum(result, -reach), reach).astype(dtype)


def setup_inputs(seed: int = 0) -> dict:
    splits = jax.random.split(jax.random.key(seed), 6)
    return {
        "grad": scatter_about(splits[0], (D, D), 1.0, 6.0, ((0, 8), (1, 96))),
        "left_rows": scatter_about(splits[1], (D, D), D ** -0.5, 0.109375, ((0, 96), (1, 8))),
        "right_basis": scatter_about(splits[2], (D, D), D ** -0.5, 0.109375, ((0, 96), (1, 8))),
        "first": scatter_about(splits[3], (D, D), 1.0, 6.0, ((0, 8), (1, 96)), jnp.float32),
        "second": jnp.clip(jnp.exp(math.log(4.0) - 4.3820266 * jax.random.uniform(splits[4], (D, D), jnp.float32) ** levels(splits[4], (D, D), ((0, 8), (1, 96)), -0.2, 0.2)), 0.05, 4.0),
    }


def blocked(left, right):
    height = left.shape[0]
    width = right.shape[1]
    lhs = left.astype(jnp.float32).reshape(height, N_ROW, -1)
    rhs = right.astype(jnp.float32).reshape(N_ROW, -1, width)
    parts = jnp.einsum('ark,rkb->rab', lhs, rhs)
    parts = lax.optimization_barrier(parts.astype(jnp.bfloat16))
    return lax.optimization_barrier(jnp.sum(parts.astype(jnp.float32), axis=0)).astype(jnp.bfloat16)

def reference(grad, left_rows, right_basis, first, second):
    mixed = blocked(left_rows, grad)
    rotated = jnp.einsum('ij,jl->li', mixed.astype(jnp.float32), right_basis.astype(jnp.float32))
    first_out = 0.9 * first + 0.1 * rotated
    second_out = 0.95 * second + 0.05 * rotated * rotated
    direction = (first_out / (jnp.sqrt(second_out) + 1e-08)).astype(jnp.bfloat16)
    back = blocked(right_basis, direction)
    update = jnp.einsum('ji,ik->kj', back.astype(jnp.float32), left_rows.astype(jnp.float32))
    return (update.astype(jnp.bfloat16), first_out, second_out)
```

```python
import jax
import jax.numpy as jnp
from jax import lax
from jax.experimental import pallas as pl
from jax.experimental.pallas import tpu as pltpu
from jax.sharding import PartitionSpec as P

MESH = pl.DeviceIdType.MESH
X, Y, Z = 4, 4, 12
F32, BF16 = jnp.float32, jnp.bfloat16
NT = (((1,), (1,)), ((), ()))

ROW_OFFSETS = [(1, 2), (1, 1), (1, 3), (1, 0), (0, 2), (0, 1), (0, 3)]
C2_OFFSETS = [(1, 2), (0, 2), (1, 1), (0, 1), (1, 3), (0, 3), (1, 0)]
Z_OFFSETS = [6, 5, 7, 4, 8, 3, 9, 2, 10, 1, 11]


def kernel(
    grad, left, right, first, second,
    update, first_out, second_out,
    lb, gb, rb, ms, mr, mf, rs, rr, df, bs, br, bf, us, ur,
    l_send, l_recv, g_send, g_recv, r_send, r_recv,
    m_send, m_recv, mf_send, mf_recv, rot_send, rot_recv,
    d_send, d_recv, b_send, b_recv, bf_send, bf_recv, u_send, u_recv,
):
    row = lax.axis_index("row")
    col = lax.axis_index("col")
    x, y_hi = lax.rem(row, X), row // X
    core, chip = lax.rem(col, 2), col // 2
    z, y_lo = lax.rem(chip, Z), chip // Z

    def row_partner(e, d):
        return lax.rem(y_hi + e, 2) * X + lax.rem(x + d, X)

    def at_row(r):
        return {"row": r, "col": col}

    def at_c2(e, a):
        c = (lax.rem(y_lo + a + Y, Y) * Z + z) * 2 + lax.rem(core + e, 2)
        return {"row": row, "col": c}

    def at_z(p):
        return {"row": row, "col": (y_lo * Z + lax.rem(z + p + Z, Z)) * 2 + core}

    def send(src, dst, send_sem, recv_sem, device):
        copy = pltpu.make_async_remote_copy(
            src_ref=src, dst_ref=dst, send_sem=send_sem, recv_sem=recv_sem,
            device_id=device, device_id_type=MESH,
        )
        copy.start()
        return copy

    barrier = pltpu.get_barrier_semaphore()
    for p in Z_OFFSETS:
        pl.semaphore_signal(barrier, inc=1, device_id=at_z(p), device_id_type=MESH)
    for e, d in ROW_OFFSETS:
        pl.semaphore_signal(barrier, inc=1, device_id=at_row(row_partner(e, d)), device_id_type=MESH)
    for e, a in C2_OFFSETS:
        pl.semaphore_signal(barrier, inc=1, device_id=at_c2(e, a), device_id_type=MESH)
    gb[0] = grad[...]
    lb[0] = left[...]
    rb[0] = right[...]
    pl.semaphore_wait(barrier, len(Z_OFFSETS) + len(ROW_OFFSETS) + len(C2_OFFSETS))

    pending = []

    g_copies = [send(gb.at[0], gb.at[p], g_send.at[p], g_recv.at[p], at_z(-p)) for p in Z_OFFSETS]
    l_copies = [
        send(lb.at[0], lb.at[e * Y + a], l_send.at[e * Y + a], l_recv.at[e * Y + a], at_c2(e, -a))
        for e, a in C2_OFFSETS
    ]
    for copy in l_copies + g_copies:
        copy.wait_recv()
    pending += l_copies + g_copies

    part = lax.dot_general(
        lb[...].reshape(256, 384), gb[...].reshape(384, 384), NT, preferred_element_type=F32
    )
    ms[...] = part.astype(BF16).reshape(8, 32, 384)
    copies = [
        send(ms.at[row_partner(e, d)], mr.at[e * X + d], m_send.at[e * X + d], m_recv.at[e * X + d],
             at_row(row_partner(e, d)))
        for e, d in ROW_OFFSETS
    ]
    r_copies = [send(rb.at[0], rb.at[p], r_send.at[p], r_recv.at[p], at_z(-p)) for p in Z_OFFSETS]
    mr[0] = ms[row]
    for copy in copies:
        copy.wait_recv()
    pending += copies
    mf[row] = jnp.sum(mr[...].astype(F32), axis=0).astype(BF16)
    copies = [
        send(mf.at[row], mf.at[row], mf_send.at[e * X + d], mf_recv.at[e * X + d],
             at_row(row_partner(e, -d + X)))
        for e, d in ROW_OFFSETS
    ]
    for copy in r_copies + copies:
        copy.wait_recv()
    pending += r_copies + copies

    part = jnp.dot(mf[...].reshape(256, 384), rb[...].reshape(384, 384), preferred_element_type=F32)
    rs[...] = part.astype(BF16).reshape(8, 32, 384)
    copies = [
        send(rs.at[e * Y + a], rr.at[e * Y + a], rot_send.at[e * Y + a], rot_recv.at[e * Y + a], at_c2(e, a))
        for e, a in C2_OFFSETS
    ]
    rr[0] = rs[0]
    for copy in copies:
        copy.wait_recv()
    pending += copies
    rotated = jnp.sum(rr[...].astype(F32), axis=0)
    m1 = 0.9 * first[...] + 0.1 * rotated
    m2 = 0.95 * second[...] + 0.05 * rotated * rotated
    df[0] = (m1 / (jnp.sqrt(m2) + 1e-08)).astype(BF16)
    copies = [
        send(df.at[0], df.at[e * Y + a], d_send.at[e * Y + a], d_recv.at[e * Y + a], at_c2(e, -a))
        for e, a in C2_OFFSETS
    ]
    first_out[...] = m1
    second_out[...] = m2
    for copy in copies:
        copy.wait_recv()
    pending += copies

    part = lax.dot_general(
        rb[...].reshape(384, 384), df[...].reshape(256, 384), NT, preferred_element_type=F32
    )
    bs[...] = part.astype(BF16).reshape(8, 48, 256)
    copies = [
        send(bs.at[row_partner(e, d)], br.at[e * X + d], b_send.at[e * X + d], b_recv.at[e * X + d],
             at_row(row_partner(e, d)))
        for e, d in ROW_OFFSETS
    ]
    br[0] = bs[row]
    for copy in copies:
        copy.wait_recv()
    pending += copies
    bf[row] = jnp.sum(br[...].astype(F32), axis=0).astype(BF16)
    copies = [
        send(bf.at[row], bf.at[row], bf_send.at[e * X + d], bf_recv.at[e * X + d],
             at_row(row_partner(e, -d + X)))
        for e, d in ROW_OFFSETS
    ]
    for copy in copies:
        copy.wait_recv()
    pending += copies

    part = jnp.dot(bf[...].reshape(384, 256), lb[...].reshape(256, 384), preferred_element_type=F32)
    us[...] = part.astype(BF16).reshape(Z, 32, 384)
    copies = [send(us.at[p], ur.at[p], u_send.at[p], u_recv.at[p], at_z(p)) for p in Z_OFFSETS]
    ur[0] = us[0]
    for copy in copies:
        copy.wait_recv()
    pending += copies
    update[...] = jnp.sum(ur[...].astype(F32), axis=0).astype(BF16)
    for copy in pending:
        copy.wait_send()


def body(grad, left, right, first, second):
    tile = (32, 384)
    def tiles(n):
        return pltpu.VMEM((n,) + tile, BF16)
    sem8, sem12 = pltpu.SemaphoreType.DMA((8,)), pltpu.SemaphoreType.DMA((Z,))
    vmem = pl.BlockSpec(memory_space=pltpu.VMEM)
    update, first_out, second_out = pl.pallas_call(
        kernel,
        out_shape=(
            jax.ShapeDtypeStruct(tile, BF16),
            jax.ShapeDtypeStruct(tile, F32),
            jax.ShapeDtypeStruct(tile, F32),
        ),
        in_specs=[vmem] * 5,
        out_specs=(vmem,) * 3,
        scratch_shapes=[
            tiles(8), tiles(Z), tiles(Z), tiles(8), tiles(8), tiles(8), tiles(8), tiles(8), tiles(8),
            pltpu.VMEM((8, 48, 256), BF16), pltpu.VMEM((8, 48, 256), BF16), pltpu.VMEM((8, 48, 256), BF16),
            tiles(Z), tiles(Z),
            sem8, sem8, sem12, sem12, sem12, sem12,
            sem8, sem8, sem8, sem8, sem8, sem8,
            sem8, sem8, sem8, sem8, sem8, sem8, sem12, sem12,
        ],
        compiler_params=pltpu.CompilerParams(
            collective_id=0, has_side_effects=True, vmem_limit_bytes=32 << 20
        ),
    )(grad.T, left, right, first.T, second.T)
    return update.T, first_out.T, second_out.T


def solution(mesh):
    placed = (P("row", "col"), P("col", "row"), P("col", "row"), P("row", "col"), P("row", "col"))
    return jax.shard_map(
        body,
        mesh=mesh,
        in_specs=placed,
        out_specs=(P("row", "col"), P("row", "col"), P("row", "col")),
        check_vma=False,
    )
```

```python
import jax
import jax.numpy as jnp
from jax import lax
from jax.experimental import pallas as pl
from jax.experimental.pallas import tpu as pltpu
from jax.sharding import PartitionSpec as P

MESH = pl.DeviceIdType.MESH
X, Y, Z = 4, 4, 12
F32, BF16 = jnp.float32, jnp.bfloat16
NT = (((1,), (1,)), ((), ()))
TN = (((0,), (0,)), ((), ()))

AFAR = (4, 8)


def kernel(
    grad, left, right, first, second,
    update, first_out, second_out,
    g_own, gq, lb, rb, mt, rs0, rs1, rx, ry_out, ry, df, bs, br, us, um, uo, ur, m1_in, m2_in,
    in_sem, ga_send, ga_recv, g_send, g_recv, la_send, la_recv, lx_send, lx_recv, core_send, core_recv,
    ra_send, ra_recv, ry_send, ry_recv, r_send, r_recv, m_send, m_recv, rot_send, rot_recv,
    d_send, d_recv, b_send, b_recv, u_send, u_recv, ua_send, ua_recv,
):
    row = lax.axis_index("row")
    col = lax.axis_index("col")
    x, y_hi = lax.rem(row, X), row // X
    core, chip = lax.rem(col, 2), col // 2
    z, y_lo = lax.rem(chip, Z), chip // Z
    other = 1 - y_hi

    local = [
        pltpu.make_async_copy(src, dst, in_sem.at[i])
        for i, (src, dst) in enumerate(
            [(grad, g_own.at[0]), (left, lb.at[0, x, 0]), (right, rb.at[y_hi, 0, 0]), (first, m1_in), (second, m2_in)]
        )
    ]
    for copy in local:
        copy.start()

    def at_zx(p, to_x):
        return {"row": y_hi * X + to_x, "col": (y_lo * Z + lax.rem(z + p + Z, Z)) * 2 + core}

    def at_x(d):
        return {"row": y_hi * X + lax.rem(x + d + X, X), "col": col}

    def at_y(h, a):
        return {"row": h * X + x, "col": (lax.rem(y_lo + a + Y, Y) * Z + z) * 2 + core}

    def at_core():
        return {"row": row, "col": chip * 2 + 1 - core}

    sent = []

    def send(src, dst, send_sem, recv_sem, device, keep=True):
        copy = pltpu.make_async_remote_copy(
            src_ref=src, dst_ref=dst, send_sem=send_sem, recv_sem=recv_sem,
            device_id=device, device_id_type=MESH,
        )
        copy.start()
        if keep:
            sent.append(copy)

    def described(ref, sem):
        return pltpu.make_async_remote_copy(
            src_ref=ref, dst_ref=ref, send_sem=sem, recv_sem=sem, device_id=at_core(), device_id_type=MESH
        )

    def wait_recv(ref, sem):
        described(ref, sem).wait_recv()

    def wait_send(ref, sem):
        described(ref, sem).wait_send()

    def near(to_x):
        if isinstance(to_x, int):
            return (0, 1, 2 - 4 * core, -1)[to_x]
        return jnp.where(to_x == 3, -1, jnp.where(to_x == 2, 2 - 4 * core, to_x))

    def y_partners():
        return [(1, other, a) for a in (2, 1, 3, 0)] + [(0, y_hi, a) for a in (2, 1, 3)]

    barrier = pltpu.get_barrier_semaphore()

    def greet(device):
        pl.semaphore_signal(barrier, inc=1, device_id=device, device_id_type=MESH)

    my_near = near(x)
    for p in AFAR:
        greet(at_zx(p, x))
    for d in (2, 1, 3):
        greet(at_zx(-near(d), d))
        greet(at_zx(my_near, lax.rem(x + d, X)))

    @pl.when(x != 0)
    def _():
        greet(at_zx(0, 0))
        greet(at_zx(my_near, x))

    for _, h, a in y_partners():
        greet(at_y(h, a))
    for n in (1, 2, 3):
        greet(at_zx(near(n), x))
    for d in (2, 1, 3):
        greet(at_x(d))
    greet(at_core())
    for copy in local:
        copy.wait()
    pl.semaphore_wait(barrier, 22 + 2 * jnp.minimum(x, 1))


    for i, p in enumerate(AFAR):
        send(g_own.at[0], g_own.at[i + 1], ga_send.at[i], ga_recv.at[i], at_zx(-p, x))
    for a in (2, 1, 3):
        send(lb.at[0, x, 0], lb.at[0, x, a], la_send.at[a], la_recv.at[a], at_y(y_hi, -a))
    for i, p in enumerate(AFAR):
        send(rb.at[y_hi, 0, 0], rb.at[y_hi, 0, i + 1], ra_send.at[i], ra_recv.at[i], at_zx(-p, x))

    for i in range(2):
        wait_recv(g_own.at[i + 1], ga_recv.at[i])
    for d in (2, 1, 3):
        send(g_own, gq.at[x], g_send.at[d], g_recv.at[x], at_zx(-near(d), d))

    @pl.when(x != 0)
    def _():
        send(g_own, gq.at[x], g_send.at[0], g_recv.at[x], at_zx(0, 0), keep=False)

    @pl.when(x == 0)
    def _():
        gq[0] = g_own[...]

    for a in (1, 2, 3):
        wait_recv(lb.at[0, x, a], la_recv.at[a])
    for d in (2, 1, 3):
        send(lb.at[0, x], lb.at[0, x], lx_send.at[d], lx_recv.at[d], at_x(-d))

    def right_near(h):
        for n in (2, 1, 3):
            send(rb.at[h, 0], rb.at[h, n], r_send.at[h, n], r_recv.at[h, n], at_zx(-near(n), x))

    for i in range(2):
        wait_recv(rb.at[y_hi, 0, i + 1], ra_recv.at[i])
    send(rb.at[y_hi, 0], rb.at[y_hi, 0], ry_send, ry_recv, at_y(other, 0))
    right_near(y_hi)
    for d in (1, 2, 3):
        wait_recv(lb.at[0, lax.rem(x + d, X)], lx_recv.at[d])
    send(lb.at[0], lb.at[1], core_send.at[0], core_recv.at[0], at_core())
    wait_recv(rb.at[other, 0], ry_recv)
    right_near(other)
    for d in (1, 2, 3):
        wait_recv(gq.at[d], g_recv.at[d])

    @pl.when(x != 0)
    def _():
        wait_recv(gq.at[0], g_recv.at[0])

    wait_recv(lb.at[1], core_recv.at[0])

    def right_gathered():
        for h in (y_hi, other):
            for n in (1, 2, 3):
                wait_recv(rb.at[h, n], r_recv.at[h, n])

    def left_of(d):
        return lb[:, d].reshape(256, 384)

    part = lax.dot_general(gq[0].reshape(96, 384), left_of(0), NT, preferred_element_type=F32)
    for d in range(1, X):
        part += lax.dot_general(gq[d].reshape(96, 384), left_of(d), NT, preferred_element_type=F32)
    mt[x] = part.astype(BF16)
    for d in (2, 1, 3):
        send(mt.at[x], mt.at[x], m_send.at[d], m_recv.at[d], at_x(-d))
    right_gathered()
    for d in (1, 2, 3):
        wait_recv(mt.at[lax.rem(x + d, X)], m_recv.at[d])

    mixed = mt[...].reshape(384, 256)
    for h in (0, 1):
        part = lax.dot_general(
            mixed[:, 128:], rb[h].reshape(384, 384), TN, preferred_element_type=F32
        )
        rs1[h] = part.astype(BF16).reshape(4, 32, 384)
    send(rs1, rx, core_send.at[1], core_recv.at[1], at_core())
    for h in (0, 1):
        rs0[h] = lax.dot_general(
            mixed[:, :128], rb[h].reshape(384, 384), TN, preferred_element_type=F32
        ).reshape(4, 32, 384)
    wait_recv(rx, core_recv.at[1])
    ry_out[...] = (rs0[...] + rx[...].astype(F32)).astype(BF16)
    for e, h, a in y_partners():
        i = e * Y + a
        send(ry_out.at[h, a], ry.at[i], rot_send.at[i], rot_recv.at[i], at_y(h, a))
    ry[0] = ry_out[y_hi, 0]
    for i in range(1, 8):
        wait_recv(ry.at[i], rot_recv.at[i])
    rotated = jnp.sum(ry[...].astype(F32), axis=0)
    m1 = 0.9 * m1_in[...] + 0.1 * rotated
    m2 = 0.95 * m2_in[...] + 0.05 * rotated * rotated
    df[0, y_hi, 0] = (m1 / (jnp.sqrt(m2) + 1e-08)).astype(BF16)
    for e, h, a in y_partners():
        i = e * Y + a
        send(df.at[0, y_hi, 0], df.at[0, y_hi, a], d_send.at[i], d_recv.at[i], at_y(h, -a))
    first_out[...] = m1
    second_out[...] = m2
    for e, h in ((0, y_hi), (1, other)):
        for a in range(Y):
            if (e, a) != (0, 0):
                wait_recv(df.at[0, h, a], d_recv.at[e * Y + a])
        send(df.at[0, h], df.at[1, h], core_send.at[2 + e], core_recv.at[2 + e], at_core())

    for e in (0, 1):
        if e == 1:
            wait_recv(df.at[1, y_hi], core_recv.at[2])
            wait_recv(df.at[1, other], core_recv.at[3])
        part = lax.dot_general(
            rb[0].reshape(384, 384), df[e, 0].reshape(128, 384), NT, preferred_element_type=F32
        ) + lax.dot_general(
            rb[1].reshape(384, 384), df[e, 1].reshape(128, 384), NT, preferred_element_type=F32
        )
        bs[:, :, 128 * e : 128 * e + 128] = part.astype(BF16).reshape(4, 96, 128)
    for d in (2, 1, 3):
        send(bs.at[lax.rem(x + d, X)], br.at[d], b_send.at[d], b_recv.at[d], at_x(d))
    br[0] = bs[x]
    for d in (1, 2, 3):
        wait_recv(br.at[d], b_recv.at[d])
    back = jnp.sum(br[...].astype(F32), axis=0).astype(BF16)

    def update_tiles(d, keep=True):
        send(us.at[d], um.at[x], u_send.at[d], u_recv.at[x], at_zx(my_near, lax.rem(x + d, X)), keep)

    for d in (2, 1, 3, 0):
        part = jnp.dot(back, left_of(lax.rem(x + d, X)), preferred_element_type=F32)
        us[d] = part.astype(BF16).reshape(3, 32, 384)
        if d:
            update_tiles(d)

    @pl.when(x != 0)
    def _():
        update_tiles(0, keep=False)
        wait_recv(um.at[0], u_recv.at[0])

    @pl.when(x == 0)
    def _():
        um[0] = us[0]

    for d in (1, 2, 3):
        wait_recv(um.at[d], u_recv.at[d])
    for i in (1, 2):
        uo[i] = jnp.sum(um[:, i].astype(F32), axis=0).astype(BF16)
        send(uo.at[i], ur.at[i], ua_send.at[i], ua_recv.at[i], at_zx(AFAR[i - 1], x))
    total = jnp.sum(um[:, 0].astype(F32), axis=0)
    for i in (1, 2):
        wait_recv(ur.at[i], ua_recv.at[i])
    update[...] = (total + ur[1].astype(F32) + ur[2].astype(F32)).astype(BF16)
    for copy in sent:
        copy.wait_send()

    @pl.when(x != 0)
    def _():
        wait_send(g_own, g_send.at[0])
        wait_send(us.at[0], u_send.at[0])


def body(grad, left, right, first, second):
    tile = (32, 384)

    def tiles(*n, dtype=BF16):
        return pltpu.VMEM(n + tile, dtype)

    def sems(*n):
        return pltpu.SemaphoreType.DMA(n)

    vmem = pl.BlockSpec(memory_space=pltpu.VMEM)
    hbm = pl.BlockSpec(memory_space=pltpu.HBM)
    update, first_out, second_out = pl.pallas_call(
        kernel,
        out_shape=(
            jax.ShapeDtypeStruct(tile, BF16),
            jax.ShapeDtypeStruct(tile, F32),
            jax.ShapeDtypeStruct(tile, F32),
        ),
        in_specs=[hbm] * 5,
        out_specs=(vmem,) * 3,
        scratch_shapes=[
            tiles(3), tiles(4, 3), tiles(2, 4, 4), tiles(2, 4, 3), pltpu.VMEM((4, 96, 256), BF16),
            tiles(2, 4, dtype=F32), tiles(2, 4), tiles(2, 4), tiles(2, 4), tiles(8), tiles(2, 2, 4),
            pltpu.VMEM((4, 96, 256), BF16), pltpu.VMEM((4, 96, 256), BF16),
            tiles(4, 3), tiles(4, 3), tiles(3), tiles(3), tiles(dtype=F32), tiles(dtype=F32),
            sems(5), sems(2), sems(2), sems(4), sems(4), sems(4), sems(4), sems(4), sems(4), sems(4), sems(4),
            sems(2), sems(2), pltpu.SemaphoreType.DMA, pltpu.SemaphoreType.DMA, sems(2, 4), sems(2, 4), sems(4), sems(4),
            sems(8), sems(8), sems(8), sems(8), sems(4), sems(4), sems(4), sems(4), sems(3), sems(3),
        ],
        compiler_params=pltpu.CompilerParams(
            collective_id=0, has_side_effects=True, vmem_limit_bytes=60 << 20
        ),
    )(grad.T, left, right, first.T, second.T)
    return update.T, first_out.T, second_out.T


def solution(mesh):
    placed = (P("row", "col"), P("col", "row"), P("col", "row"), P("row", "col"), P("row", "col"))
    return jax.shard_map(
        body,
        mesh=mesh,
        in_specs=placed,
        out_specs=(P("row", "col"), P("row", "col"), P("row", "col")),
        check_vma=False,
    )
```

```python
import jax
import jax.numpy as jnp
from jax import lax
from jax.experimental import pallas as pl
from jax.experimental.pallas import tpu as pltpu
from jax.sharding import PartitionSpec as P

MESH = pl.DeviceIdType.MESH
X, Y, Z = 4, 4, 12
F32, BF16 = jnp.float32, jnp.bfloat16
NT = (((1,), (1,)), ((), ()))
TN = (((0,), (0,)), ((), ()))

AFAR = (4, 8)


def kernel(
    grad, left, right, first, second,
    update, first_out, second_out,
    g_own, gq, lb, rb, mt, rs0, rs1, rx, ry_out, ry, df, bs, br, us, um, uo, ur, m1_in, m2_in,
    in_sem, ga_send, ga_recv, g_send, g_recv, la_send, la_recv, lx_send, lx_recv, lc_send, lc_recv, core_send, core_recv,
    ra_send, ra_recv, ry_send, ry_recv, r_send, r_recv, m_send, m_recv, rot_send, rot_recv,
    d_send, d_recv, b_send, b_recv, u_send, u_recv, ua_send, ua_recv,
):
    row = lax.axis_index("row")
    col = lax.axis_index("col")
    x, y_hi = lax.rem(row, X), row // X
    core, chip = lax.rem(col, 2), col // 2
    z, y_lo = lax.rem(chip, Z), chip // Z
    other = 1 - y_hi

    local = [
        pltpu.make_async_copy(src, dst, in_sem.at[i])
        for i, (src, dst) in enumerate(
            [(grad, g_own.at[0]), (left, lb.at[0, x, 0]), (right, rb.at[y_hi, 0, 0]), (first, m1_in), (second, m2_in)]
        )
    ]
    for copy in local:
        copy.start()

    def at_zx(p, to_x):
        return {"row": y_hi * X + to_x, "col": (y_lo * Z + lax.rem(z + p + Z, Z)) * 2 + core}

    def at_x(d):
        return {"row": y_hi * X + lax.rem(x + d + X, X), "col": col}

    def at_y(h, a):
        return {"row": h * X + x, "col": (lax.rem(y_lo + a + Y, Y) * Z + z) * 2 + core}

    def at_core():
        return {"row": row, "col": chip * 2 + 1 - core}

    sent = []

    def send(src, dst, send_sem, recv_sem, device, keep=True):
        copy = pltpu.make_async_remote_copy(
            src_ref=src, dst_ref=dst, send_sem=send_sem, recv_sem=recv_sem,
            device_id=device, device_id_type=MESH,
        )
        copy.start()
        if keep:
            sent.append(copy)

    def described(ref, sem):
        return pltpu.make_async_remote_copy(
            src_ref=ref, dst_ref=ref, send_sem=sem, recv_sem=sem, device_id=at_core(), device_id_type=MESH
        )

    def wait_recv(ref, sem):
        described(ref, sem).wait_recv()

    def wait_send(ref, sem):
        described(ref, sem).wait_send()

    def near(to_x):
        if isinstance(to_x, int):
            return (0, 1, 2 - 4 * core, -1)[to_x]
        return jnp.where(to_x == 3, -1, jnp.where(to_x == 2, 2 - 4 * core, to_x))

    def y_partners():
        return [(1, other, a) for a in (0, 2, 1, 3)] + [(0, y_hi, a) for a in (2, 1, 3)]

    barrier = pltpu.get_barrier_semaphore()

    def greet(device):
        pl.semaphore_signal(barrier, inc=1, device_id=device, device_id_type=MESH)

    my_near = near(x)
    for p in AFAR:
        greet(at_zx(p, x))
    for d in (2, 1, 3):
        greet(at_zx(-near(d), d))
        greet(at_zx(my_near, lax.rem(x + d, X)))

    @pl.when(x != 0)
    def _():
        greet(at_zx(0, 0))
        greet(at_zx(my_near, x))

    for _, h, a in y_partners():
        greet(at_y(h, a))
    for n in (1, 2, 3):
        greet(at_zx(near(n), x))
    for d in (2, 1, 3):
        greet(at_x(d))
    greet(at_core())
    for copy in local:
        copy.wait()
    pl.semaphore_wait(barrier, 22 + 2 * jnp.minimum(x, 1))


    for a in (2, 1, 3):
        send(lb.at[0, x, 0], lb.at[0, x, a], la_send.at[a], la_recv.at[a], at_y(y_hi, -a))
    for i, p in enumerate(AFAR):
        send(g_own.at[0], g_own.at[i + 1], ga_send.at[i], ga_recv.at[i], at_zx(-p, x))
    for i, p in enumerate(AFAR):
        send(rb.at[y_hi, 0, 0], rb.at[y_hi, 0, i + 1], ra_send.at[i], ra_recv.at[i], at_zx(-p, x))

    def left_to_core(d):
        mine = lb.at[0, lax.rem(x + d, X)]
        send(mine, lb.at[1, lax.rem(x + d, X)], lc_send.at[d], lc_recv.at[d], at_core())

    for a in (1, 2, 3):
        wait_recv(lb.at[0, x, a], la_recv.at[a])
    for d in (2, 1, 3):
        send(lb.at[0, x], lb.at[0, x], lx_send.at[d], lx_recv.at[d], at_x(-d))
    left_to_core(0)

    for i in range(2):
        wait_recv(g_own.at[i + 1], ga_recv.at[i])
    for d in (2, 1, 3):
        send(g_own, gq.at[x], g_send.at[d], g_recv.at[x], at_zx(-near(d), d))

    @pl.when(x != 0)
    def _():
        send(g_own, gq.at[x], g_send.at[0], g_recv.at[x], at_zx(0, 0), keep=False)

    @pl.when(x == 0)
    def _():
        gq[0] = g_own[...]

    def right_near(h):
        for n in (2, 1, 3):
            send(rb.at[h, 0], rb.at[h, n], r_send.at[h, n], r_recv.at[h, n], at_zx(-near(n), x))

    for i in range(2):
        wait_recv(rb.at[y_hi, 0, i + 1], ra_recv.at[i])
    send(rb.at[y_hi, 0], rb.at[y_hi, 0], ry_send, ry_recv, at_y(other, 0))
    right_near(y_hi)
    for d in (1, 3, 2):
        wait_recv(lb.at[0, lax.rem(x + d, X)], lx_recv.at[d])
        left_to_core(d)
    wait_recv(rb.at[other, 0], ry_recv)
    right_near(other)
    for d in (1, 2, 3):
        wait_recv(gq.at[d], g_recv.at[d])

    @pl.when(x != 0)
    def _():
        wait_recv(gq.at[0], g_recv.at[0])

    for d in range(X):
        wait_recv(lb.at[1, lax.rem(x + d, X)], lc_recv.at[d])

    def right_gathered():
        for h in (y_hi, other):
            for n in (1, 2, 3):
                wait_recv(rb.at[h, n], r_recv.at[h, n])

    def left_of(d):
        return lb[:, d].reshape(256, 384)

    part = lax.dot_general(gq[0].reshape(96, 384), left_of(0), NT, preferred_element_type=F32)
    for d in range(1, X):
        part += lax.dot_general(gq[d].reshape(96, 384), left_of(d), NT, preferred_element_type=F32)
    mt[x] = part.astype(BF16)
    for d in (2, 1, 3):
        send(mt.at[x], mt.at[x], m_send.at[d], m_recv.at[d], at_x(-d))
    right_gathered()
    for d in (1, 2, 3):
        wait_recv(mt.at[lax.rem(x + d, X)], m_recv.at[d])

    mixed = mt[...].reshape(384, 256)
    for h in (0, 1):
        part = lax.dot_general(
            mixed[:, 128:], rb[h].reshape(384, 384), TN, preferred_element_type=F32
        )
        rs1[h] = part.astype(BF16).reshape(4, 32, 384)
    send(rs1, rx, core_send.at[1], core_recv.at[1], at_core())
    for h in (0, 1):
        rs0[h] = lax.dot_general(
            mixed[:, :128], rb[h].reshape(384, 384), TN, preferred_element_type=F32
        ).reshape(4, 32, 384)
    wait_recv(rx, core_recv.at[1])
    ry_out[...] = (rs0[...] + rx[...].astype(F32)).astype(BF16)
    for e, h, a in y_partners():
        i = e * Y + a
        send(ry_out.at[h, a], ry.at[i], rot_send.at[i], rot_recv.at[i], at_y(h, a))
    ry[0] = ry_out[y_hi, 0]
    for i in range(1, 8):
        wait_recv(ry.at[i], rot_recv.at[i])
    rotated = jnp.sum(ry[...].astype(F32), axis=0)
    m1 = 0.9 * m1_in[...] + 0.1 * rotated
    m2 = 0.95 * m2_in[...] + 0.05 * rotated * rotated
    df[0, y_hi, 0] = (m1 / (jnp.sqrt(m2) + 1e-08)).astype(BF16)
    for e, h, a in y_partners():
        i = e * Y + a
        send(df.at[0, y_hi, 0], df.at[0, y_hi, a], d_send.at[i], d_recv.at[i], at_y(h, -a))
    first_out[...] = m1
    second_out[...] = m2
    for e, h in ((0, y_hi), (1, other)):
        for a in range(Y):
            if (e, a) != (0, 0):
                wait_recv(df.at[0, h, a], d_recv.at[e * Y + a])
        send(df.at[0, h], df.at[1, h], core_send.at[2 + e], core_recv.at[2 + e], at_core())

    for e in (0, 1):
        if e == 1:
            wait_recv(df.at[1, y_hi], core_recv.at[2])
            wait_recv(df.at[1, other], core_recv.at[3])
        part = lax.dot_general(
            rb[0].reshape(384, 384), df[e, 0].reshape(128, 384), NT, preferred_element_type=F32
        ) + lax.dot_general(
            rb[1].reshape(384, 384), df[e, 1].reshape(128, 384), NT, preferred_element_type=F32
        )
        bs[:, :, 128 * e : 128 * e + 128] = part.astype(BF16).reshape(4, 96, 128)
    for d in (2, 1, 3):
        send(bs.at[lax.rem(x + d, X)], br.at[d], b_send.at[d], b_recv.at[d], at_x(d))
    br[0] = bs[x]
    for d in (1, 2, 3):
        wait_recv(br.at[d], b_recv.at[d])
    back = jnp.sum(br[...].astype(F32), axis=0).astype(BF16)

    def update_tiles(d, keep=True):
        send(us.at[d], um.at[x], u_send.at[d], u_recv.at[x], at_zx(my_near, lax.rem(x + d, X)), keep)

    for d in (2, 1, 3, 0):
        part = jnp.dot(back, left_of(lax.rem(x + d, X)), preferred_element_type=F32)
        us[d] = part.astype(BF16).reshape(3, 32, 384)
        if d:
            update_tiles(d)

    @pl.when(x != 0)
    def _():
        update_tiles(0, keep=False)
        wait_recv(um.at[0], u_recv.at[0])

    @pl.when(x == 0)
    def _():
        um[0] = us[0]

    for d in (1, 2, 3):
        wait_recv(um.at[d], u_recv.at[d])
    for i in (1, 2):
        uo[i] = jnp.sum(um[:, i].astype(F32), axis=0).astype(BF16)
        send(uo.at[i], ur.at[i], ua_send.at[i], ua_recv.at[i], at_zx(AFAR[i - 1], x))
    total = jnp.sum(um[:, 0].astype(F32), axis=0)
    for i in (1, 2):
        wait_recv(ur.at[i], ua_recv.at[i])
    update[...] = (total + ur[1].astype(F32) + ur[2].astype(F32)).astype(BF16)
    for copy in sent:
        copy.wait_send()

    @pl.when(x != 0)
    def _():
        wait_send(g_own, g_send.at[0])
        wait_send(us.at[0], u_send.at[0])


def body(grad, left, right, first, second):
    tile = (32, 384)

    def tiles(*n, dtype=BF16):
        return pltpu.VMEM(n + tile, dtype)

    def sems(*n):
        return pltpu.SemaphoreType.DMA(n)

    vmem = pl.BlockSpec(memory_space=pltpu.VMEM)
    hbm = pl.BlockSpec(memory_space=pltpu.HBM)
    update, first_out, second_out = pl.pallas_call(
        kernel,
        out_shape=(
            jax.ShapeDtypeStruct(tile, BF16),
            jax.ShapeDtypeStruct(tile, F32),
            jax.ShapeDtypeStruct(tile, F32),
        ),
        in_specs=[hbm] * 5,
        out_specs=(vmem,) * 3,
        scratch_shapes=[
            tiles(3), tiles(4, 3), tiles(2, 4, 4), tiles(2, 4, 3), pltpu.VMEM((4, 96, 256), BF16),
            tiles(2, 4, dtype=F32), tiles(2, 4), tiles(2, 4), tiles(2, 4), tiles(8), tiles(2, 2, 4),
            pltpu.VMEM((4, 96, 256), BF16), pltpu.VMEM((4, 96, 256), BF16),
            tiles(4, 3), tiles(4, 3), tiles(3), tiles(3), tiles(dtype=F32), tiles(dtype=F32),
            sems(5), sems(2), sems(2), sems(4), sems(4), sems(4), sems(4), sems(4), sems(4), sems(4), sems(4), sems(4), sems(4),
            sems(2), sems(2), pltpu.SemaphoreType.DMA, pltpu.SemaphoreType.DMA, sems(2, 4), sems(2, 4), sems(4), sems(4),
            sems(8), sems(8), sems(8), sems(8), sems(4), sems(4), sems(4), sems(4), sems(3), sems(3),
        ],
        compiler_params=pltpu.CompilerParams(
            collective_id=0, has_side_effects=True, vmem_limit_bytes=60 << 20
        ),
    )(grad.T, left, right, first.T, second.T)
    return update.T, first_out.T, second_out.T


def solution(mesh):
    placed = (P("row", "col"), P("col", "row"), P("col", "row"), P("row", "col"), P("row", "col"))
    return jax.shard_map(
        body,
        mesh=mesh,
        in_specs=placed,
        out_specs=(P("row", "col"), P("row", "col"), P("row", "col")),
        check_vma=False,
    )
```

```python
import jax
import jax.numpy as jnp
from jax import lax
from jax.experimental import pallas as pl
from jax.experimental.pallas import tpu as pltpu
from jax.sharding import PartitionSpec as P

MESH = pl.DeviceIdType.MESH
X, Y, Z = 4, 4, 12
F32, BF16 = jnp.float32, jnp.bfloat16
NT = (((1,), (1,)), ((), ()))
TN = (((0,), (0,)), ((), ()))

AFAR = (4, 8)


def kernel(
    grad, left, right, first, second,
    update, first_out, second_out,
    g_own, gq, lb, rb, mt, rs0, rs1, rx, ry_out, ry, df, bs, br, back, us, um, uo, ur, m1_in, m2_in,
    in_sem, ga_send, ga_recv, g_send, g_recv, la_send, la_recv, lx_send, lx_recv, lc_send, lc_recv, core_send, core_recv,
    ra_send, ra_recv, ry_send, ry_recv, r_send, r_recv, m_send, m_recv, rot_send, rot_recv,
    d_send, d_recv, b_send, b_recv, u_send, u_recv, ua_send, ua_recv,
):
    row = lax.axis_index("row")
    col = lax.axis_index("col")
    x, y_hi = lax.rem(row, X), row // X
    core, chip = lax.rem(col, 2), col // 2
    z, y_lo = lax.rem(chip, Z), chip // Z
    other = 1 - y_hi

    local = [
        pltpu.make_async_copy(src, dst, in_sem.at[i])
        for i, (src, dst) in enumerate(
            [(grad, g_own.at[0]), (left, lb.at[0, x, 0]), (right, rb.at[y_hi, 0, 0]), (first, m1_in), (second, m2_in)]
        )
    ]
    for copy in local:
        copy.start()

    def at_zx(p, to_x):
        return {"row": y_hi * X + to_x, "col": (y_lo * Z + lax.rem(z + p + Z, Z)) * 2 + core}

    def at_x(d):
        return {"row": y_hi * X + lax.rem(x + d + X, X), "col": col}

    def at_y(h, a):
        return {"row": h * X + x, "col": (lax.rem(y_lo + a + Y, Y) * Z + z) * 2 + core}

    def at_core():
        return {"row": row, "col": chip * 2 + 1 - core}

    sent = []

    def send(src, dst, send_sem, recv_sem, device, keep=True):
        copy = pltpu.make_async_remote_copy(
            src_ref=src, dst_ref=dst, send_sem=send_sem, recv_sem=recv_sem,
            device_id=device, device_id_type=MESH,
        )
        copy.start()
        if keep:
            sent.append(copy)

    def described(ref, sem):
        return pltpu.make_async_remote_copy(
            src_ref=ref, dst_ref=ref, send_sem=sem, recv_sem=sem, device_id=at_core(), device_id_type=MESH
        )

    def wait_recv(ref, sem):
        described(ref, sem).wait_recv()

    def wait_send(ref, sem):
        described(ref, sem).wait_send()

    def near(to_x):
        if isinstance(to_x, int):
            return (0, 1, 2 - 4 * core, -1)[to_x]
        return jnp.where(to_x == 3, -1, jnp.where(to_x == 2, 2 - 4 * core, to_x))

    def y_partners():
        return [(1, other, a) for a in (0, 2, 1, 3)] + [(0, y_hi, a) for a in (2, 1, 3)]

    barrier = pltpu.get_barrier_semaphore()

    def greet(device):
        pl.semaphore_signal(barrier, inc=1, device_id=device, device_id_type=MESH)

    my_near = near(x)
    for p in AFAR:
        greet(at_zx(p, x))
    for d in (2, 1, 3):
        greet(at_zx(-near(d), d))
        greet(at_zx(my_near, lax.rem(x + d, X)))

    @pl.when(x != 0)
    def _():
        greet(at_zx(0, 0))
        greet(at_zx(my_near, x))

    for _, h, a in y_partners():
        greet(at_y(h, a))
    for n in (1, 2, 3):
        greet(at_zx(near(n), x))
    for d in (2, 1, 3):
        greet(at_x(d))
    greet(at_core())
    for copy in local:
        copy.wait()
    pl.semaphore_wait(barrier, 22 + 2 * jnp.minimum(x, 1))


    for a in (2, 1, 3):
        send(lb.at[0, x, 0], lb.at[0, x, a], la_send.at[a], la_recv.at[a], at_y(y_hi, -a))
    for i, p in enumerate(AFAR):
        send(g_own.at[0], g_own.at[i + 1], ga_send.at[i], ga_recv.at[i], at_zx(-p, x))
    for i, p in enumerate(AFAR):
        send(rb.at[y_hi, 0, 0], rb.at[y_hi, 0, i + 1], ra_send.at[i], ra_recv.at[i], at_zx(-p, x))

    def left_to_core(d):
        mine = lb.at[0, lax.rem(x + d, X)]
        send(mine, lb.at[1, lax.rem(x + d, X)], lc_send.at[d], lc_recv.at[d], at_core())

    for a in (1, 2, 3):
        wait_recv(lb.at[0, x, a], la_recv.at[a])
    for d in (2, 1, 3):
        send(lb.at[0, x], lb.at[0, x], lx_send.at[d], lx_recv.at[d], at_x(-d))
    left_to_core(0)

    for i in range(2):
        wait_recv(g_own.at[i + 1], ga_recv.at[i])
    for d in (2, 1, 3):
        send(g_own, gq.at[x], g_send.at[d], g_recv.at[x], at_zx(-near(d), d))

    @pl.when(x != 0)
    def _():
        send(g_own, gq.at[x], g_send.at[0], g_recv.at[x], at_zx(0, 0), keep=False)

    @pl.when(x == 0)
    def _():
        gq[0] = g_own[...]

    def right_near(h):
        for n in (2, 1, 3):
            send(rb.at[h, 0], rb.at[h, n], r_send.at[h, n], r_recv.at[h, n], at_zx(-near(n), x))

    for i in range(2):
        wait_recv(rb.at[y_hi, 0, i + 1], ra_recv.at[i])
    send(rb.at[y_hi, 0], rb.at[y_hi, 0], ry_send, ry_recv, at_y(other, 0))
    right_near(y_hi)
    for d in (1, 3, 2):
        wait_recv(lb.at[0, lax.rem(x + d, X)], lx_recv.at[d])
        left_to_core(d)
    wait_recv(rb.at[other, 0], ry_recv)
    right_near(other)
    def right_gathered():
        for h in (y_hi, other):
            for n in (1, 2, 3):
                wait_recv(rb.at[h, n], r_recv.at[h, n])

    def left_of(d):
        return lb[:, d].reshape(256, 384)

    @pl.when(x != 0)
    def _():
        wait_recv(gq.at[x], g_recv.at[x])

    part = jnp.zeros((96, 256), F32)
    for d in (0, 1, 3, 2):
        source = lax.rem(x + d, X)
        if d:
            wait_recv(gq.at[source], g_recv.at[source])
        wait_recv(lb.at[1, source], lc_recv.at[d])
        part += lax.dot_general(gq[source].reshape(96, 384), left_of(source), NT, preferred_element_type=F32)
    mt[x] = part.astype(BF16)
    for d in (2, 1, 3):
        send(mt.at[x], mt.at[x], m_send.at[d], m_recv.at[d], at_x(-d))
    right_gathered()
    for d in (1, 2, 3):
        wait_recv(mt.at[lax.rem(x + d, X)], m_recv.at[d])

    mixed = mt[...].reshape(384, 256)
    for h in (0, 1):
        part = lax.dot_general(
            mixed[:, 128:], rb[h].reshape(384, 384), TN, preferred_element_type=F32
        )
        rs1[h] = part.astype(BF16).reshape(4, 32, 384)
    send(rs1, rx, core_send.at[1], core_recv.at[1], at_core())
    for h in (0, 1):
        rs0[h] = lax.dot_general(
            mixed[:, :128], rb[h].reshape(384, 384), TN, preferred_element_type=F32
        ).reshape(4, 32, 384)
    wait_recv(rx, core_recv.at[1])
    ry_out[...] = (rs0[...] + rx[...].astype(F32)).astype(BF16)
    for e, h, a in y_partners():
        i = e * Y + a
        send(ry_out.at[h, a], ry.at[i], rot_send.at[i], rot_recv.at[i], at_y(h, a))
    ry[0] = ry_out[y_hi, 0]
    for i in range(1, 8):
        wait_recv(ry.at[i], rot_recv.at[i])
    rotated = jnp.sum(ry[...].astype(F32), axis=0)
    m1 = 0.9 * m1_in[...] + 0.1 * rotated
    m2 = 0.95 * m2_in[...] + 0.05 * rotated * rotated
    df[0, y_hi, 0] = (m1 / (jnp.sqrt(m2) + 1e-08)).astype(BF16)
    for e, h, a in y_partners():
        i = e * Y + a
        send(df.at[0, y_hi, 0], df.at[0, y_hi, a], d_send.at[i], d_recv.at[i], at_y(h, -a))
    first_out[...] = m1
    second_out[...] = m2
    for e, h in ((0, y_hi), (1, other)):
        for a in range(Y):
            if (e, a) != (0, 0):
                wait_recv(df.at[0, h, a], d_recv.at[e * Y + a])
        send(df.at[0, h], df.at[1, h], core_send.at[2 + e], core_recv.at[2 + e], at_core())

    for e in (0, 1):
        if e == 1:
            wait_recv(df.at[1, y_hi], core_recv.at[2])
            wait_recv(df.at[1, other], core_recv.at[3])
        part = lax.dot_general(
            rb[0].reshape(384, 384), df[e, 0].reshape(128, 384), NT, preferred_element_type=F32
        ) + lax.dot_general(
            rb[1].reshape(384, 384), df[e, 1].reshape(128, 384), NT, preferred_element_type=F32
        )
        bs[e] = part.astype(BF16).reshape(4, 96, 128)
        for d in (2, 1, 3):
            send(bs.at[e, lax.rem(x + d, X)], br.at[e, d], b_send.at[e, d], b_recv.at[e, d], at_x(d))
        br[e, 0] = bs[e, x]
    for e in (0, 1):
        for d in (1, 2, 3):
            wait_recv(br.at[e, d], b_recv.at[e, d])
        back[:, 128 * e : 128 * e + 128] = jnp.sum(br[e].astype(F32), axis=0).astype(BF16)

    def update_tiles(d, keep=True):
        send(us.at[d], um.at[x], u_send.at[d], u_recv.at[x], at_zx(my_near, lax.rem(x + d, X)), keep)

    for d in (2, 1, 3, 0):
        part = jnp.dot(back[...], left_of(lax.rem(x + d, X)), preferred_element_type=F32)
        us[d] = part.astype(BF16).reshape(3, 32, 384)
        if d:
            update_tiles(d)

    @pl.when(x != 0)
    def _():
        update_tiles(0, keep=False)
        wait_recv(um.at[0], u_recv.at[0])

    @pl.when(x == 0)
    def _():
        um[0] = us[0]

    for d in (1, 2, 3):
        wait_recv(um.at[d], u_recv.at[d])
    for i in (1, 2):
        uo[i] = jnp.sum(um[:, i].astype(F32), axis=0).astype(BF16)
        send(uo.at[i], ur.at[i], ua_send.at[i], ua_recv.at[i], at_zx(AFAR[i - 1], x))
    total = jnp.sum(um[:, 0].astype(F32), axis=0)
    for i in (1, 2):
        wait_recv(ur.at[i], ua_recv.at[i])
    update[...] = (total + ur[1].astype(F32) + ur[2].astype(F32)).astype(BF16)
    for copy in sent:
        copy.wait_send()

    @pl.when(x != 0)
    def _():
        wait_send(g_own, g_send.at[0])
        wait_send(us.at[0], u_send.at[0])


def body(grad, left, right, first, second):
    tile = (32, 384)

    def tiles(*n, dtype=BF16):
        return pltpu.VMEM(n + tile, dtype)

    def sems(*n):
        return pltpu.SemaphoreType.DMA(n)

    vmem = pl.BlockSpec(memory_space=pltpu.VMEM)
    hbm = pl.BlockSpec(memory_space=pltpu.HBM)
    update, first_out, second_out = pl.pallas_call(
        kernel,
        out_shape=(
            pltpu.VMEM(tile, BF16),
            pltpu.VMEM(tile, F32),
            pltpu.VMEM(tile, F32),
        ),
        in_specs=[hbm] * 5,
        out_specs=(vmem,) * 3,
        scratch_shapes=[
            tiles(3), tiles(4, 3), tiles(2, 4, 4), tiles(2, 4, 3), pltpu.VMEM((4, 96, 256), BF16),
            tiles(2, 4, dtype=F32), tiles(2, 4), tiles(2, 4), tiles(2, 4), tiles(8), tiles(2, 2, 4),
            pltpu.VMEM((2, 4, 96, 128), BF16), pltpu.VMEM((2, 4, 96, 128), BF16), pltpu.VMEM((96, 256), BF16),
            tiles(4, 3), tiles(4, 3), tiles(3), tiles(3), tiles(dtype=F32), tiles(dtype=F32),
            sems(5), sems(2), sems(2), sems(4), sems(4), sems(4), sems(4), sems(4), sems(4), sems(4), sems(4), sems(4), sems(4),
            sems(2), sems(2), pltpu.SemaphoreType.DMA, pltpu.SemaphoreType.DMA, sems(2, 4), sems(2, 4), sems(4), sems(4),
            sems(8), sems(8), sems(8), sems(8), sems(2, 4), sems(2, 4), sems(4), sems(4), sems(3), sems(3),
        ],
        compiler_params=pltpu.CompilerParams(
            collective_id=0, has_side_effects=True, vmem_limit_bytes=60 << 20
        ),
    )(grad.T, left, right, first.T, second.T)
    return update.T, first_out.T, second_out.T


def solution(mesh):
    placed = (P("row", "col"), P("col", "row"), P("col", "row"), P("row", "col"), P("row", "col"))
    return jax.shard_map(
        body,
        mesh=mesh,
        in_specs=placed,
        out_specs=(P("row", "col"), P("row", "col"), P("row", "col")),
        check_vma=False,
    )
```

```python
import jax
import jax.numpy as jnp
from jax import lax
from jax.experimental import pallas as pl
from jax.experimental.pallas import tpu as pltpu
from jax.sharding import PartitionSpec as P

MESH = pl.DeviceIdType.MESH
X, Y, Z = 4, 4, 12
F32, BF16 = jnp.float32, jnp.bfloat16
NT = (((1,), (1,)), ((), ()))
TN = (((0,), (0,)), ((), ()))

AFAR = (4, 8)


def kernel(
    grad, left, right, first, second,
    update, first_out, second_out,
    g_own, gq, lb, rb, mt, rs0, rs1, rx, ry_out, ry, df, bs, br, back, up, us, um, uo, ur, m1_in, m2_in,
    in_sem, ga_send, ga_recv, g_send, g_recv, la_send, la_recv, lx_send, lx_recv, lc_send, lc_recv, core_send, core_recv,
    rx_send, rx_recv, ra_send, ra_recv, ry_send, ry_recv, r_send, r_recv, m_send, m_recv, rot_send, rot_recv,
    d_send, d_recv, b_send, b_recv, u_send, u_recv, ua_send, ua_recv,
):
    row = lax.axis_index("row")
    col = lax.axis_index("col")
    x, y_hi = lax.rem(row, X), row // X
    core, chip = lax.rem(col, 2), col // 2
    z, y_lo = lax.rem(chip, Z), chip // Z
    other = 1 - y_hi

    local = [
        pltpu.make_async_copy(src, dst, in_sem.at[i])
        for i, (src, dst) in enumerate(
            [(grad, g_own.at[0]), (left, lb.at[0, x, 0]), (right, rb.at[y_hi, 0, 0]), (first, m1_in), (second, m2_in)]
        )
    ]
    for copy in local:
        copy.start()

    def at_zx(p, to_x):
        return {"row": y_hi * X + to_x, "col": (y_lo * Z + lax.rem(z + p + Z, Z)) * 2 + core}

    def at_x(d):
        return {"row": y_hi * X + lax.rem(x + d + X, X), "col": col}

    def at_y(h, a):
        return {"row": h * X + x, "col": (lax.rem(y_lo + a + Y, Y) * Z + z) * 2 + core}

    def at_core():
        return {"row": row, "col": chip * 2 + 1 - core}

    sent = []

    def send(src, dst, send_sem, recv_sem, device, keep=True):
        copy = pltpu.make_async_remote_copy(
            src_ref=src, dst_ref=dst, send_sem=send_sem, recv_sem=recv_sem,
            device_id=device, device_id_type=MESH,
        )
        copy.start()
        if keep:
            sent.append(copy)

    def described(ref, sem):
        return pltpu.make_async_remote_copy(
            src_ref=ref, dst_ref=ref, send_sem=sem, recv_sem=sem, device_id=at_core(), device_id_type=MESH
        )

    def wait_recv(ref, sem):
        described(ref, sem).wait_recv()

    def wait_send(ref, sem):
        described(ref, sem).wait_send()

    def near(to_x):
        if isinstance(to_x, int):
            return (0, 1, 2 - 4 * core, -1)[to_x]
        return jnp.where(to_x == 3, -1, jnp.where(to_x == 2, 2 - 4 * core, to_x))

    def y_partners():
        return [(1, other, a) for a in (0, 2, 1, 3)] + [(0, y_hi, a) for a in (2, 1, 3)]

    barrier = pltpu.get_barrier_semaphore()

    def greet(device):
        pl.semaphore_signal(barrier, inc=1, device_id=device, device_id_type=MESH)

    my_near = near(x)
    for p in AFAR:
        greet(at_zx(p, x))
    for d in (2, 1, 3):
        greet(at_zx(-near(d), d))
        greet(at_zx(my_near, lax.rem(x + d, X)))

    @pl.when(x != 0)
    def _():
        greet(at_zx(0, 0))
        greet(at_zx(my_near, x))

    for _, h, a in y_partners():
        greet(at_y(h, a))
    for n in (1, 2, 3):
        greet(at_zx(near(n), x))
    for d in (2, 1, 3):
        greet(at_x(d))
    greet(at_core())
    for copy in local:
        copy.wait()
    pl.semaphore_wait(barrier, 22 + 2 * jnp.minimum(x, 1))


    for a in (2, 1, 3):
        send(lb.at[0, x, 0], lb.at[0, x, a], la_send.at[a], la_recv.at[a], at_y(y_hi, -a))
    for i, p in enumerate(AFAR):
        send(g_own.at[0], g_own.at[i + 1], ga_send.at[i], ga_recv.at[i], at_zx(-p, x))
    for i, p in enumerate(AFAR):
        send(rb.at[y_hi, 0, 0], rb.at[y_hi, 0, i + 1], ra_send.at[i], ra_recv.at[i], at_zx(-p, x))

    def left_to_core(d):
        mine = lb.at[0, lax.rem(x + d, X)]
        send(mine, lb.at[1, lax.rem(x + d, X)], lc_send.at[d], lc_recv.at[d], at_core())

    for a in (1, 2, 3):
        wait_recv(lb.at[0, x, a], la_recv.at[a])
    for d in (2, 1, 3):
        send(lb.at[0, x], lb.at[0, x], lx_send.at[d], lx_recv.at[d], at_x(-d))
    left_to_core(0)

    for i in range(2):
        wait_recv(g_own.at[i + 1], ga_recv.at[i])
    for d in (2, 1, 3):
        send(g_own, gq.at[x], g_send.at[d], g_recv.at[x], at_zx(-near(d), d))

    @pl.when(x != 0)
    def _():
        send(g_own, gq.at[x], g_send.at[0], g_recv.at[x], at_zx(0, 0), keep=False)

    @pl.when(x == 0)
    def _():
        gq[0] = g_own[...]

    def right_near(h):
        for n in (2, 1, 3):
            send(rb.at[h, 0], rb.at[h, n], r_send.at[h, n], r_recv.at[h, n], at_zx(-near(n), x))

    for i in range(2):
        wait_recv(rb.at[y_hi, 0, i + 1], ra_recv.at[i])
    send(rb.at[y_hi, 0], rb.at[y_hi, 0], ry_send, ry_recv, at_y(other, 0))
    right_near(y_hi)
    for d in (1, 3, 2):
        wait_recv(lb.at[0, lax.rem(x + d, X)], lx_recv.at[d])
        left_to_core(d)
    wait_recv(rb.at[other, 0], ry_recv)
    right_near(other)
    def right_gathered(h):
        for n in (1, 2, 3):
            wait_recv(rb.at[h, n], r_recv.at[h, n])

    def left_of(d):
        return lb[:, d].reshape(256, 384)

    @pl.when(x != 0)
    def _():
        wait_recv(gq.at[x], g_recv.at[x])

    part = jnp.zeros((96, 256), F32)
    for d in (0, 1, 3, 2):
        source = lax.rem(x + d, X)
        if d:
            wait_recv(gq.at[source], g_recv.at[source])
        wait_recv(lb.at[1, source], lc_recv.at[d])
        part += lax.dot_general(gq[source].reshape(96, 384), left_of(source), NT, preferred_element_type=F32)
    mt[x] = part.astype(BF16)
    for d in (2, 1, 3):
        send(mt.at[x], mt.at[x], m_send.at[d], m_recv.at[d], at_x(-d))
    for d in (1, 2, 3):
        wait_recv(mt.at[lax.rem(x + d, X)], m_recv.at[d])

    mixed = mt[...].reshape(384, 256)
    parts = ((1, other), (0, y_hi))

    def rotated_of(columns, h):
        return lax.dot_general(
            columns, rb[h].reshape(384, 384), TN, preferred_element_type=F32
        ).reshape(4, 32, 384)

    for e, h in parts:
        right_gathered(h)
        rs1[h] = rotated_of(mixed[:, 128:], h).astype(BF16)
        send(rs1.at[h], rx.at[h], rx_send.at[e], rx_recv.at[e], at_core())
    for e, h in parts:
        rs0[h] = rotated_of(mixed[:, :128], h)
        wait_recv(rx.at[h], rx_recv.at[e])
        ry_out[h] = (rs0[h] + rx[h].astype(F32)).astype(BF16)
        for f, _, a in y_partners():
            if f == e:
                i = e * Y + a
                send(ry_out.at[h, a], ry.at[i], rot_send.at[i], rot_recv.at[i], at_y(h, a))
    ry[0] = ry_out[y_hi, 0]
    for i in range(1, 8):
        wait_recv(ry.at[i], rot_recv.at[i])
    rotated = jnp.sum(ry[...].astype(F32), axis=0)
    m1 = 0.9 * m1_in[...] + 0.1 * rotated
    m2 = 0.95 * m2_in[...] + 0.05 * rotated * rotated
    df[0, y_hi, 0] = (m1 / (jnp.sqrt(m2) + 1e-08)).astype(BF16)
    for e, h, a in y_partners():
        i = e * Y + a
        send(df.at[0, y_hi, 0], df.at[0, y_hi, a], d_send.at[i], d_recv.at[i], at_y(h, -a))
    first_out[...] = m1
    second_out[...] = m2
    for e, h in ((0, y_hi), (1, other)):
        for a in range(Y):
            if (e, a) != (0, 0):
                wait_recv(df.at[0, h, a], d_recv.at[e * Y + a])
        send(df.at[0, h], df.at[1, h], core_send.at[2 + e], core_recv.at[2 + e], at_core())

    for e in (0, 1):
        if e == 1:
            wait_recv(df.at[1, y_hi], core_recv.at[2])
            wait_recv(df.at[1, other], core_recv.at[3])
        part = lax.dot_general(
            rb[0].reshape(384, 384), df[e, 0].reshape(128, 384), NT, preferred_element_type=F32
        ) + lax.dot_general(
            rb[1].reshape(384, 384), df[e, 1].reshape(128, 384), NT, preferred_element_type=F32
        )
        bs[e] = part.astype(BF16).reshape(4, 96, 128)
        for d in (2, 1, 3):
            send(bs.at[e, lax.rem(x + d, X)], br.at[e, d], b_send.at[e, d], b_recv.at[e, d], at_x(d))
        br[e, 0] = bs[e, x]

    def update_tiles(d, keep=True):
        send(us.at[d], um.at[x], u_send.at[d], u_recv.at[x], at_zx(my_near, lax.rem(x + d, X)), keep)

    for e in (0, 1):
        for d in (1, 2, 3):
            wait_recv(br.at[e, d], b_recv.at[e, d])
        back[e] = jnp.sum(br[e].astype(F32), axis=0).astype(BF16)
        if e == 0:
            for d in range(X):
                up[d] = jnp.dot(back[0], lb[0, d].reshape(128, 384), preferred_element_type=F32)
    for d in (2, 1, 3, 0):
        to_x = lax.rem(x + d, X)
        part = up[to_x] + jnp.dot(back[1], lb[1, to_x].reshape(128, 384), preferred_element_type=F32)
        us[d] = part.astype(BF16).reshape(3, 32, 384)
        if d:
            update_tiles(d)

    @pl.when(x != 0)
    def _():
        update_tiles(0, keep=False)
        wait_recv(um.at[0], u_recv.at[0])

    @pl.when(x == 0)
    def _():
        um[0] = us[0]

    for d in (1, 2, 3):
        wait_recv(um.at[d], u_recv.at[d])
    for i in (1, 2):
        uo[i] = jnp.sum(um[:, i].astype(F32), axis=0).astype(BF16)
        send(uo.at[i], ur.at[i], ua_send.at[i], ua_recv.at[i], at_zx(AFAR[i - 1], x))
    total = jnp.sum(um[:, 0].astype(F32), axis=0)
    for i in (1, 2):
        wait_recv(ur.at[i], ua_recv.at[i])
    update[...] = (total + ur[1].astype(F32) + ur[2].astype(F32)).astype(BF16)
    for copy in sent:
        copy.wait_send()

    @pl.when(x != 0)
    def _():
        wait_send(g_own, g_send.at[0])
        wait_send(us.at[0], u_send.at[0])


def body(grad, left, right, first, second):
    tile = (32, 384)

    def tiles(*n, dtype=BF16):
        return pltpu.VMEM(n + tile, dtype)

    def sems(*n):
        return pltpu.SemaphoreType.DMA(n)

    vmem = pl.BlockSpec(memory_space=pltpu.VMEM)
    hbm = pl.BlockSpec(memory_space=pltpu.HBM)
    update, first_out, second_out = pl.pallas_call(
        kernel,
        out_shape=(
            pltpu.VMEM(tile, BF16),
            pltpu.VMEM(tile, F32),
            pltpu.VMEM(tile, F32),
        ),
        in_specs=[hbm] * 5,
        out_specs=(vmem,) * 3,
        scratch_shapes=[
            tiles(3), tiles(4, 3), tiles(2, 4, 4), tiles(2, 4, 3), pltpu.VMEM((4, 96, 256), BF16),
            tiles(2, 4, dtype=F32), tiles(2, 4), tiles(2, 4), tiles(2, 4), tiles(8), tiles(2, 2, 4),
            pltpu.VMEM((2, 4, 96, 128), BF16), pltpu.VMEM((2, 4, 96, 128), BF16), pltpu.VMEM((2, 96, 128), BF16), pltpu.VMEM((4, 96, 384), F32),
            tiles(4, 3), tiles(4, 3), tiles(3), tiles(3), tiles(dtype=F32), tiles(dtype=F32),
            sems(5), sems(2), sems(2), sems(4), sems(4), sems(4), sems(4), sems(4), sems(4), sems(4), sems(4), sems(4), sems(4),
            sems(2), sems(2), sems(2), sems(2), pltpu.SemaphoreType.DMA, pltpu.SemaphoreType.DMA, sems(2, 4), sems(2, 4), sems(4), sems(4),
            sems(8), sems(8), sems(8), sems(8), sems(2, 4), sems(2, 4), sems(4), sems(4), sems(3), sems(3),
        ],
        compiler_params=pltpu.CompilerParams(
            collective_id=0, has_side_effects=True, vmem_limit_bytes=60 << 20
        ),
    )(grad.T, left, right, first.T, second.T)
    return update.T, first_out.T, second_out.T


def solution(mesh):
    placed = (P("row", "col"), P("col", "row"), P("col", "row"), P("row", "col"), P("row", "col"))
    return jax.shard_map(
        body,
        mesh=mesh,
        in_specs=placed,
        out_specs=(P("row", "col"), P("row", "col"), P("row", "col")),
        check_vma=False,
    )
```
